32 devices in a mesh: groups: 2 (over y), ha: 4 (over z), ta: 2 (over x), col: 2 (over core).
Axes of the slice: x: 2, y: 2, z: 4, core: 2. Of those that a mesh axis runs over, the one named last changes fastest.
Arguments:
- tokens: bfloat16 [8, 16, 64, 768], P(('groups', 'ta'), 'ha', None, 'col'), parts along dimension 0, may hold values from -6 to 6
- norm1_gain: float32 [768], replicated, may hold values from 0.4 to 1.6
- w_qkv: bfloat16 [3, 768, 768], P(None, None, 'col'), may hold values from -0.21875 to 0.21875
- w_out: bfloat16 [768, 768], P('col'), may hold values from -0.3125 to 0.3125
- norm2_gain: float32 [768], replicated, may hold values from 0.4 to 1.6
- w_up: bfloat16 [768, 3072], P('ha', 'col'), may hold values from -0.21875 to 0.21875
- w_down: bfloat16 [3072, 768], P('col', 'ha'), may hold values from -0.109375 to 0.109375
Outputs:
- block_out: bfloat16 [8, 16, 64, 768], P(('groups', 'ta'), 'ha', None, 'col'), parts along dimension 0
The draws below stay inside these ranges and needn't reach their ends.
There are 2 independent parts, one for each index of `groups`. The reference program is written for one: setup_inputs(seed, part) draws one part's arguments, and reference() takes and returns one part's arrays. A program takes and returns all parts, laid end to end along the dimension named above; an argument that names none is the same for every part. Nothing has to cross between parts.
All inputs are finite; a program needn't handle non-finite values.
Results may differ from the reference program's by a relative error of at most 0.009.
Values may be sent and summed in bfloat16 or wider, within the bound.
A program may use at most 64 MiB of HBM per device.

```python
import math
import jax
import jax.numpy as jnp
from jax import lax

HD = 64
FF = 3072
W = 64
D = 768
FRAMES = 4
HEIGHT = 16


def level_of(rng, shape, cuts, smallest, high):
    factor_of, own = 1.0, jax.random.fold_in(rng, 6)
    for axis_at, blocks in cuts:
        draws = jnp.exp(jax.random.uniform(jax.random.fold_in(own, axis_at), (blocks,), jnp.float32, smallest / len(cuts), high / len(cuts)))
        factor_of = factor_of * jnp.repeat(draws, shape[axis_at] // blocks).reshape([-1 if axis == axis_at else 1 for axis in range(len(shape))])
    return factor_of


def normal_values(own_key, shape, deviation, reach, pieces=(), dtype=jnp.bfloat16):
    drawn = deviation * jax.random.normal(own_key, shape, jnp.float32)
    if pieces:
        drawn = drawn * level_of(own_key, shape, pieces, -0.22, 0.18)
    return jnp.clip(drawn, -reach, reach).astype(dtype)


def setup_inputs(seed: int = 0, part: int = 0) -> dict:
    arg_keys = jax.random.split(jax.random.key(seed), 8)
    part_splits = jax.random.split(jax.random.fold_in(arg_keys[7], part), 8)
    tokens = normal_values(part_splits[0], (FRAMES, HEIGHT, W, D), 1.0, 6.0, ((0, 2), (1, 4), (3, 2)))
    norm1_gain = jnp.clip(1.0 + 0.12 * jax.random.normal(arg_keys[1], (D,), jnp.float32), 0.4, 1.6)
    w_qkv = normal_values(arg_keys[2], (3, D, D), D ** -0.5, 0.21875, ((2, 2),))
    w_out = normal_values(arg_keys[3], (D, D), (D // 2) ** -0.5, 0.3125, ((0, 2),))
    norm2_gain = jnp.clip(1.0 + 0.12 * jax.random.normal(arg_keys[4], (D,), jnp.float32), 0.4, 1.6)
    w_up = normal_values(arg_keys[5], (D, FF), D ** -0.5, 0.21875, ((0, 4), (1, 2)))
    w_down = normal_values(arg_keys[6], (FF, D), FF ** -0.5, 0.109375, ((0, 2), (1, 4)))
    return dict(tokens=tokens, norm1_gain=norm1_gain, w_qkv=w_qkv, w_out=w_out, norm2_gain=norm2_gain, w_up=w_up, w_down=w_down)


EPS = 1e-05

def layer_norm(values, gain):
    mean = lax.optimization_barrier(jnp.mean(values, -1, keepdims=True))
    centred = values - mean
    spread = lax.optimization_barrier(jnp.mean(centred * centred, -1, keepdims=True))
    return centred * lax.rsqrt(spread + EPS) * gain.astype(jnp.float32)

def attend(query, keys, values, dim):
    scale = 1.0 / math.sqrt(HD)
    moved_q = jnp.moveaxis(query, dim, -2)
    moved_k = jnp.moveaxis(keys, dim, -2)
    moved_v = jnp.moveaxis(values, dim, -2)
    shape = moved_q.shape
    split = shape[:-1] + (shape[-1] // HD, HD)
    heads_q = moved_q.reshape(split).astype(jnp.float32)
    heads_k = moved_k.reshape(split).astype(jnp.float32)
    heads_v = moved_v.reshape(split).astype(jnp.float32)
    scores = jnp.einsum('...qhd,...khd->...hqk', heads_q, heads_k) * scale
    weights = jnp.exp(scores)
    weights = weights / lax.optimization_barrier(jnp.sum(weights, -1, keepdims=True))
    weights = weights.astype(jnp.bfloat16).astype(jnp.float32)
    result = jnp.einsum('...hqk,...khd->...qhd', weights, heads_v).astype(jnp.bfloat16)
    return jnp.moveaxis(result.reshape(shape), -2, dim)

def reference(tokens, norm1_gain, w_qkv, w_out, norm2_gain, w_up, w_down):
    frames, height, width, model = tokens.shape
    wide = tokens.astype(jnp.float32).reshape(-1, model)
    normed = layer_norm(wide, norm1_gain).astype(jnp.bfloat16)
    query = jnp.dot(normed, w_qkv[0], preferred_element_type=jnp.float32).astype(jnp.bfloat16).reshape(tokens.shape)
    keys = jnp.dot(normed, w_qkv[1], preferred_element_type=jnp.float32).astype(jnp.bfloat16).reshape(tokens.shape)
    values = jnp.dot(normed, w_qkv[2], preferred_element_type=jnp.float32).astype(jnp.bfloat16).reshape(tokens.shape)
    along_w = attend(query, keys, values, 2)
    along_h = attend(query, keys, values, 1)
    along_t = attend(query, keys, values, 0)
    mixed = (along_w.astype(jnp.float32) + along_h.astype(jnp.float32) + along_t.astype(jnp.float32)).astype(jnp.bfloat16)
    first = wide + jnp.dot(mixed.reshape(-1, model), w_out, preferred_element_type=jnp.float32)
    second = layer_norm(first, norm2_gain).astype(jnp.bfloat16)

    def feed(block):
        rows_in, resid = block
        upper = jnp.dot(rows_in, w_up, preferred_element_type=jnp.float32)
        hidden = jax.nn.gelu(upper, approximate=False).astype(jnp.bfloat16)
        return (resid + jnp.dot(hidden, w_down, preferred_element_type=jnp.float32)).astype(jnp.bfloat16)
    result = lax.map(feed, (second.reshape(frames, -1, model), first.reshape(frames, -1, model)))
    return result.reshape(frames, height, width, model)
```

```python
import functools
import math

import jax
import jax.numpy as jnp
from jax import lax
from jax.experimental import pallas as pl
from jax.experimental.pallas import tpu as pltpu
from jax.sharding import PartitionSpec as P

HD = 64


EPS = 1e-05


def layer_norm(values, gain):
    mean = jnp.mean(values, -1, keepdims=True)
    centred = values - mean
    spread = jnp.mean(centred * centred, -1, keepdims=True)
    return centred * lax.rsqrt(spread + EPS) * gain


def attend(query, keys, values, dim):
    scale = 1.0 / math.sqrt(HD)
    moved_q = jnp.moveaxis(query, dim, -2)
    moved_k = jnp.moveaxis(keys, dim, -2)
    moved_v = jnp.moveaxis(values, dim, -2)
    shape = moved_q.shape
    split = shape[:-1] + (shape[-1] // HD, HD)
    scores = (
        jnp.einsum(
            "...qhd,...khd->...hqk",
            moved_q.reshape(split),
            moved_k.reshape(split),
            preferred_element_type=jnp.float32,
        )
        * scale
    )
    weights = jnp.exp(scores)
    weights = (weights / jnp.sum(weights, -1, keepdims=True)).astype(jnp.bfloat16)
    result = jnp.einsum(
        "...hqk,...khd->...qhd", weights, moved_v.reshape(split), preferred_element_type=jnp.float32
    ).astype(jnp.bfloat16)
    return jnp.moveaxis(result.reshape(shape), -2, dim)


def on_device(tokens, norm1_gain, w_qkv, w_out, norm2_gain, w_up, w_down):
    whole = lax.all_gather(tokens, "col", axis=3, tiled=True)
    frames, rows_h, width, model = whole.shape
    count = frames * rows_h * width
    half = tokens.shape[3]
    wide = whole.astype(jnp.float32).reshape(count, model)
    normed = layer_norm(wide, norm1_gain).astype(jnp.bfloat16)
    stacked = jnp.einsum("rd,sdc->src", normed, w_qkv, preferred_element_type=jnp.float32).astype(
        jnp.bfloat16
    )
    stacked = stacked.reshape(3, frames, rows_h, width, half)
    along_w = attend(stacked[0], stacked[1], stacked[2], 2)
    columns = lax.all_to_all(stacked, "ha", split_axis=3, concat_axis=2, tiled=True)
    along_h_far = attend(columns[0], columns[1], columns[2], 1)
    along_h = lax.all_to_all(along_h_far, "ha", split_axis=1, concat_axis=2, tiled=True)
    lines = lax.all_to_all(stacked, "ta", split_axis=3, concat_axis=1, tiled=True)
    along_t_far = attend(lines[0], lines[1], lines[2], 0)
    along_t = lax.all_to_all(along_t_far, "ta", split_axis=0, concat_axis=2, tiled=True)
    mixed = (
        along_w.astype(jnp.float32) + along_h.astype(jnp.float32) + along_t.astype(jnp.float32)
    ).astype(jnp.bfloat16)
    terms = jnp.dot(mixed.reshape(count, half), w_out, preferred_element_type=jnp.float32)
    offset = lax.axis_index("col") * half
    summed = lax.psum(terms, "col")
    first_full = wide + summed
    second = layer_norm(first_full, norm2_gain).astype(jnp.bfloat16)
    first = lax.dynamic_slice_in_dim(first_full, offset, half, 1)
    upper = jnp.dot(
        second, lax.all_gather(w_up, "ha", axis=0, tiled=True), preferred_element_type=jnp.float32
    )
    hidden = jax.nn.gelu(upper, approximate=False).astype(jnp.bfloat16)
    down_terms = jnp.dot(
        hidden, lax.all_gather(w_down, "ha", axis=1, tiled=True), preferred_element_type=jnp.float32
    )
    down_share = lax.psum_scatter(
        down_terms.astype(jnp.bfloat16), "col", scatter_dimension=1, tiled=True
    ).astype(jnp.float32)
    return (first + down_share).astype(jnp.bfloat16).reshape(frames, rows_h, width, half)


F32 = jnp.float32
BF = jnp.bfloat16


def norm_rows(parts, gain_ref, out_ref, rows):
    half = parts[0].shape[-1]
    model = 2 * half
    total = jnp.sum(parts[0], -1, keepdims=True) + jnp.sum(parts[1], -1, keepdims=True)
    mean = total * (1.0 / model)
    centred = [part - mean for part in parts]
    spread = sum(jnp.sum(part * part, -1, keepdims=True) for part in centred) * (1.0 / model)
    factor = lax.rsqrt(spread + EPS)
    for at, part in enumerate(centred):
        gain = gain_ref[:, at * half : (at + 1) * half]
        out_ref[rows, at * half : (at + 1) * half] = (part * factor * gain).astype(BF)


def attend_pair(query, keys, values, mask):
    count = query.shape[0]
    low = lax.broadcasted_iota(jnp.int32, query.shape, 1) < HD
    zero = jnp.zeros_like(query)
    both = jnp.concatenate([jnp.where(low, query, zero), jnp.where(low, zero, query)], 0)
    scores = lax.dot_general(both, keys, (((1,), (1,)), ((), ())), preferred_element_type=F32)
    weights = jnp.where(mask, jnp.exp(scores), 0.0)
    ones = jnp.ones((keys.shape[0], 128), BF)
    sums = jnp.dot(weights.astype(BF), ones, preferred_element_type=F32)
    probs = (weights / sums).astype(BF)
    found = jnp.dot(probs, values, preferred_element_type=F32)
    return jnp.where(low, found[:count], found[count:]).astype(BF).astype(F32)


def block_kernel(
    sizes, tok, gain1, wqkv_hbm, wout_hbm, gain2, wup_hbm, wdn_hbm, out,
    own, sendb, strip, nrm, qkv, found, heads_w, backb, back, mix, first,
    wq, wo, wu, wdl, wdp, wd, hid, downb, downr, wide,
    sem_l, s_tok, r_tok, s_col, r_col, s_fwd, r_fwd, s_ret, r_ret,
    s_z, r_z, s_p, r_p, s_mix, r_mix, s_dn, r_dn,
):
    n_g, n_ha, n_ta = sizes
    g, z, t, c = (lax.axis_index(name) for name in ("groups", "ha", "ta", "col"))
    oc = 1 - c
    me = t * n_ha + z
    half = tok.shape[2]
    quarter = t * n_g + g
    partner = {"col": oc}

    def remote(src, dst, send, recv, to):
        return pltpu.make_async_remote_copy(
            src_ref=src, dst_ref=dst, send_sem=send, recv_sem=recv,
            device_id=to, device_id_type=pl.DeviceIdType.MESH,
        )

    moves = [(dt, dz) for dt in range(n_ta) for dz in range(n_ha) if dt or dz]
    plane = [(dt, dg) for dt in range(n_ta) for dg in range(n_g) if dt or dg]

    def other(dt, dz):
        return lax.rem(t + dt, n_ta), lax.rem(z + dz, n_ha)

    barrier = pltpu.get_barrier_semaphore()
    for dt, dz in moves:
        to_t, to_z = other(dt, dz)
        pl.semaphore_signal(barrier, inc=1, device_id={"ha": to_z, "ta": to_t}, device_id_type=pl.DeviceIdType.MESH)
    pl.semaphore_signal(barrier, inc=1, device_id=partner, device_id_type=pl.DeviceIdType.MESH)
    for dt, dg in plane:
        if dg:
            to = {"groups": lax.rem(g + dg, n_g), "ta": lax.rem(t + dt, n_ta)}
            pl.semaphore_signal(barrier, inc=1, device_id=to, device_id_type=pl.DeviceIdType.MESH)

    local = [
        pltpu.make_async_copy(wdn_hbm, wdl, sem_l.at[0]),
        pltpu.make_async_copy(wqkv_hbm, wq, sem_l.at[1]),
        pltpu.make_async_copy(wout_hbm, wo.at[c], sem_l.at[2]),
        pltpu.make_async_copy(wup_hbm, wu.at[z], sem_l.at[3]),
    ]
    for copy in local:
        copy.start()

    lines = tok.shape[0]
    tokens = tok[...].astype(F32)
    narrow = tok.shape[1] // (n_ha * n_ta)
    for s in range(n_ha * n_ta):
        cut = tokens[:, s * narrow : (s + 1) * narrow, :]
        sendb[s] = cut.reshape(lines * narrow, half).astype(BF)
    own[c] = tok[...]
    strip[c, me] = sendb[me]

    n_sig = len(moves) + 1 + sum(1 for dt, dg in plane if dg)
    pl.semaphore_wait(barrier, n_sig)

    own_send = remote(own.at[c], own.at[c], s_col.at[0], r_col.at[0], partner)
    own_send.start()
    sends = []
    for at, (dt, dz) in enumerate(moves):
        to_t, to_z = other(dt, dz)
        copy = remote(sendb.at[to_t * n_ha + to_z], strip.at[c, me], s_tok.at[at], r_tok.at[at], {"ha": to_z, "ta": to_t})
        copy.start()
        sends.append(copy)
    forward = remote(strip.at[c, me], strip.at[c, me], s_fwd.at[len(moves)], r_fwd.at[len(moves)], partner)
    forward.start()
    sends.append(forward)

    z_up, z_down = [], []
    local[0].wait()
    part_rows = wdl.shape[0] // 4
    for q in range(4):
        piece = wdl[q * part_rows : (q + 1) * part_rows, :].astype(F32)
        wdp[z, q, :part_rows] = piece[:, :128].astype(BF)
        rest = piece[:, 128:]
        wdp[z, q, part_rows:] = jnp.concatenate([rest[: part_rows // 2], rest[part_rows // 2 :]], 1).astype(BF)
    for d in range(1, n_ha):
        to = {"ha": lax.rem(z + d, n_ha)}
        copy = remote(wup_hbm.at[quarter], wu.at[z, quarter], s_z.at[0, d], r_z.at[0, d], to)
        copy.start()
        z_up.append(copy)
    for d in range(1, n_ha):
        to = {"ha": lax.rem(z + d, n_ha)}
        copy = remote(wdp.at[z, quarter], wdp.at[z, quarter], s_z.at[1, d], r_z.at[1, d], to)
        copy.start()
        z_down.append(copy)
    local[1].wait()
    local[2].wait()
    wo_send = remote(wo.at[c], wo.at[c], s_col.at[1], r_col.at[1], partner)
    wo_send.start()
    sends += z_up + z_down

    def project():
        for i in range(3):
            value = jnp.dot(nrm[...], wq[i], preferred_element_type=F32)
            if i == 0:
                value = value.astype(BF).astype(F32) * (1.0 / math.sqrt(HD))
            qkv[i] = value.astype(BF).reshape(qkv.shape[1:])

    count = lines * tok.shape[1]
    block = 128
    rows_at = lax.rem(lax.broadcasted_iota(jnp.int32, (2 * block, block), 0), block)
    cols_at = lax.broadcasted_iota(jnp.int32, (2 * block, block), 1)
    pairs = half // 128

    own_send.wait()
    norm_rows(
        [own[0].reshape(count, half).astype(F32), own[1].reshape(count, half).astype(F32)],
        gain1, nrm, slice(None),
    )
    project()
    width = tok.shape[1]
    mask_w = rows_at // width == cols_at // width
    flat = qkv.reshape(3, count // block, block, half)

    def along_w(b, carry):
        for p in range(pairs):
            lanes = pl.ds(p * 128, 128)
            heads_w[b, :, lanes] = attend_pair(flat[0, b, :, lanes], flat[1, b, :, lanes], flat[2, b, :, lanes], mask_w)
        return carry

    lax.fori_loop(0, count // block, along_w, 0)

    for at, (dt, dz) in enumerate(moves):
        from_t, from_z = lax.rem(t + n_ta - dt, n_ta), lax.rem(z + n_ha - dz, n_ha)
        src = from_t * n_ha + from_z
        remote(sendb.at[0], strip.at[c, src], s_tok.at[at], r_tok.at[at], partner).wait_recv()
        copy = remote(strip.at[c, src], strip.at[c, src], s_fwd.at[at], r_fwd.at[at], partner)
        copy.start()
        sends.append(copy)
    for at, (dt, dz) in enumerate(moves + [(0, 0)]):
        from_t, from_z = lax.rem(t + n_ta - dt, n_ta), lax.rem(z + n_ha - dz, n_ha)
        src = from_t * n_ha + from_z
        remote(strip.at[oc, src], strip.at[oc, src], s_fwd.at[at], r_fwd.at[at], partner).wait_recv()
    norm_rows(
        [strip[0].reshape(count, half).astype(F32), strip[1].reshape(count, half).astype(F32)],
        gain1, nrm, slice(None),
    )
    project()
    frames = 2
    mask_h = lax.rem(rows_at, narrow) == lax.rem(cols_at, narrow)
    same = lines // frames * narrow
    mask_t = lax.rem(rows_at, same) == lax.rem(cols_at, same)

    def along_h(b, carry):
        tt, ff = b // frames, lax.rem(b, frames)
        for p in range(pairs):
            lanes = pl.ds(p * 128, 128)
            q, k, v = (qkv[i, tt, :, ff, :, lanes].reshape(block, 128) for i in range(3))
            found[tt, :, ff, :, lanes] = attend_pair(q, k, v, mask_h).reshape(n_ha, same, 128)
        return carry

    def along_t(zz, carry):
        for p in range(pairs):
            lanes = pl.ds(p * 128, 128)
            q, k, v = (qkv[i, :, zz, :, :, lanes].reshape(block, 128) for i in range(3))
            more = attend_pair(q, k, v, mask_t).reshape(n_ta, frames, same, 128)
            backb[:, zz, :, :, lanes] = (found[:, zz, :, :, lanes] + more).astype(BF)
        return carry

    lax.fori_loop(0, n_ta * frames, along_h, 0)
    lax.fori_loop(0, n_ha, along_t, 0)

    for at, (dt, dz) in enumerate(moves):
        to_t, to_z = other(dt, dz)
        copy = remote(backb.at[to_t, to_z], back.at[t, z], s_ret.at[at], r_ret.at[at], {"ha": to_z, "ta": to_t})
        copy.start()
        sends.append(copy)
    back[t, z] = backb[t, z]

    def spread(kind, buf):
        for d in range(1, n_ha):
            zz = lax.rem(z + n_ha - d, n_ha)
            remote(buf.at[zz, quarter], buf.at[zz, quarter], s_z.at[kind, d], r_z.at[kind, d], partner).wait_recv()
            for at, (dt, dg) in enumerate(plane):
                to = {"groups": lax.rem(g + dg, n_g), "ta": lax.rem(t + dt, n_ta)}
                copy = remote(buf.at[zz, quarter], buf.at[zz, quarter], s_p.at[kind, d, at], r_p.at[kind, d, at], to)
                copy.start()
                sends.append(copy)

    def spread_wait(kind, buf):
        for d in range(1, n_ha):
            zz = lax.rem(z + n_ha - d, n_ha)
            for at, (dt, dg) in enumerate(plane):
                qq = lax.rem(t + n_ta - dt, n_ta) * n_g + lax.rem(g + n_g - dg, n_g)
                remote(buf.at[zz, qq], buf.at[zz, qq], s_p.at[kind, d, at], r_p.at[kind, d, at], partner).wait_recv()

    spread(0, wu)

    for at, (dt, dz) in enumerate(moves):
        from_t, from_z = lax.rem(t + n_ta - dt, n_ta), lax.rem(z + n_ha - dz, n_ha)
        remote(back.at[from_t, from_z], back.at[from_t, from_z], s_ret.at[at], r_ret.at[at], partner).wait_recv()
    for s in range(n_ha * n_ta):
        piece = back[s // n_ha, s % n_ha].astype(F32)
        wide[:, s * narrow : (s + 1) * narrow, :] = piece.reshape(lines, narrow, half)
    mix[c] = (wide[...].reshape(count, half) + heads_w[...].reshape(count, half)).astype(BF)
    mix_send = remote(mix.at[c], mix.at[c], s_mix.at[0], r_mix.at[0], partner)
    mix_send.start()
    spread(1, wdp)
    wo_send.wait()
    first[...] = jnp.dot(mix[c], wo[c], preferred_element_type=F32)
    mix_send.wait()
    first[...] += jnp.dot(mix[oc], wo[oc], preferred_element_type=F32)
    parts = []
    for i in range(2):
        cols = slice(i * half, (i + 1) * half)
        part = own[i].reshape(count, half).astype(F32) + first[:, cols]
        first[:, cols] = part
        parts.append(part)
    norm_rows(parts, gain2, nrm, slice(None))

    local[3].wait()
    spread_wait(0, wu)
    units = wu.shape[3]
    step = 256

    def feed(u, carry):
        cols = pl.ds(pl.multiple_of(u * step, step), step)
        up = jnp.dot(nrm[...], wu[:, :, :, cols].reshape(2 * half, step), preferred_element_type=F32)
        up = 0.5 * up * (1.0 + lax.erf(up * math.sqrt(0.5)))
        hid[:, cols] = up.astype(BF)
        return carry

    lax.fori_loop(0, units // step, feed, 0)

    spread_wait(1, wdp)
    small = part_rows // 2
    low = lax.broadcasted_iota(jnp.int32, (small, 128), 1) < 64
    for q in range(4):
        for zp in range(n_ha // 2):
            lead = zp * 384
            rows = slice(q * part_rows, (q + 1) * part_rows)
            wd[rows, lead : lead + 128] = wdp[2 * zp, q, :part_rows]
            wd[rows, lead + 128 : lead + 256] = wdp[2 * zp + 1, q, :part_rows]
            even = wdp[2 * zp, q, part_rows:].astype(F32)
            odd = wdp[2 * zp + 1, q, part_rows:].astype(F32)
            wd[q * part_rows : q * part_rows + small, lead + 256 : lead + 384] = jnp.where(low, even, pltpu.roll(odd, 64, 1)).astype(BF)
            wd[q * part_rows + small : (q + 1) * part_rows, lead + 256 : lead + 384] = jnp.where(low, pltpu.roll(even, 64, 1), odd).astype(BF)

    there = pl.ds(pl.multiple_of(oc * half, 128), half)
    here = pl.ds(pl.multiple_of(c * half, 128), half)
    n_rows = 2
    tall = count // n_rows
    down = []
    for r in range(n_rows):
        rows = slice(r * tall, (r + 1) * tall)
        downb[r] = jnp.dot(hid[rows, :], wd[:, there], preferred_element_type=F32).astype(BF)
        copy = remote(downb.at[r], downr.at[r], s_dn.at[r], r_dn.at[r], partner)
        copy.start()
        down.append(copy)
    for r in range(n_rows):
        rows = slice(r * tall, (r + 1) * tall)
        mine = jnp.dot(hid[rows, :], wd[:, here], preferred_element_type=F32)
        down[r].wait_recv()
        mine = mine + downr[r].astype(F32)
        a0, a1, b = mine[:, :128], mine[:, 128:256], mine[:, 256:384]
        total = jnp.concatenate([a0, b[:, :64], a1, b[:, 64:]], 1) + first[rows, here]
        out[rows, :] = total.astype(BF)
    for copy in down + sends:
        copy.wait_send()


def on_device_fused(sizes, tokens, norm1_gain, w_qkv, w_out, norm2_gain, w_up, w_down):
    n_g, n_ha, n_ta = sizes
    frames, rows_h, width, half = tokens.shape
    lines = frames * rows_h
    count = lines * width
    strips = n_ha * n_ta
    narrow = width // strips
    same = rows_h * narrow
    units = w_up.shape[1]
    packed = units // 4 * 3 // 2
    dma = pltpu.SemaphoreType.DMA
    vm = pltpu.VMEM
    n_moves = strips - 1
    scratch = [
        vm((2, lines, width, half), BF),
        vm((strips, lines * narrow, half), BF),
        vm((2, strips, lines * narrow, half), BF),
        vm((count, 2 * half), BF),
        vm((3, n_ta, n_ha, frames, same, half), BF),
        vm((n_ta, n_ha, frames, same, half), F32),
        vm((count // 128, 128, half), F32),
        vm((n_ta, n_ha, frames, same, half), BF),
        vm((n_ta, n_ha, frames, same, half), BF),
        vm((2, count, half), BF),
        vm((count, 2 * half), F32),
        vm((3, 2 * half, half), BF),
        vm((2, half, 2 * half), BF),
        vm((n_ha, 4, w_up.shape[0] // 4, units), BF),
        vm((units, w_down.shape[1]), BF),
        vm((n_ha, 4, packed, 128), BF),
        vm((units, 2 * half), BF),
        vm((count, units), BF),
        vm((2, count // 2, half), BF),
        vm((2, count // 2, half), BF),
        vm((lines, width, half), F32),
        dma((4,)),
        dma((n_moves,)), dma((n_moves,)),
        dma((2,)), dma((2,)),
        dma((strips,)), dma((strips,)),
        dma((n_moves,)), dma((n_moves,)),
        dma((2, n_ha)), dma((2, n_ha)),
        dma((2, n_ha, 3)), dma((2, n_ha, 3)),
        dma((1,)), dma((1,)),
        dma((2,)), dma((2,)),
    ]
    in_vmem = pl.BlockSpec(memory_space=pltpu.VMEM)
    anywhere = pl.BlockSpec(memory_space=pl.ANY)
    result = pl.pallas_call(
        functools.partial(block_kernel, sizes),
        out_shape=jax.ShapeDtypeStruct((count, half), BF),
        in_specs=[in_vmem, in_vmem, anywhere, anywhere, in_vmem, anywhere, anywhere],
        out_specs=in_vmem,
        scratch_shapes=scratch,
        compiler_params=pltpu.CompilerParams(
            collective_id=0, has_side_effects=True, vmem_limit_bytes=56 * 2**20
        ),
    )(
        tokens.reshape(lines, width, half), norm1_gain.reshape(1, -1), w_qkv, w_out,
        norm2_gain.reshape(1, -1), w_up.reshape(4, w_up.shape[0] // 4, units), w_down,
    )
    return result.reshape(frames, rows_h, width, half)


def fits(mesh):
    shape = mesh.shape
    return shape["groups"] == 2 and shape["ta"] == 2 and shape["ha"] == 4 and shape["col"] == 2


def solution(mesh):
    placed = (
        P(("groups", "ta"), "ha", None, "col"),
        P(),
        P(None, None, "col"),
        P("col", None),
        P(),
        P("ha", "col"),
        P("col", "ha"),
    )
    body = on_device
    if fits(mesh):
        body = functools.partial(on_device_fused, (mesh.shape["groups"], mesh.shape["ha"], mesh.shape["ta"]))
    return jax.shard_map(
        body,
        mesh=mesh,
        in_specs=placed,
        out_specs=P(("groups", "ta"), "ha", None, "col"),
        check_vma=False,
    )
```

```python
import functools
import math

import jax
import jax.numpy as jnp
from jax import lax
from jax.experimental import pallas as pl
from jax.experimental.pallas import tpu as pltpu
from jax.sharding import PartitionSpec as P

HD = 64


EPS = 1e-05


def layer_norm(values, gain):
    mean = jnp.mean(values, -1, keepdims=True)
    centred = values - mean
    spread = jnp.mean(centred * centred, -1, keepdims=True)
    return centred * lax.rsqrt(spread + EPS) * gain


def attend(query, keys, values, dim):
    scale = 1.0 / math.sqrt(HD)
    moved_q = jnp.moveaxis(query, dim, -2)
    moved_k = jnp.moveaxis(keys, dim, -2)
    moved_v = jnp.moveaxis(values, dim, -2)
    shape = moved_q.shape
    split = shape[:-1] + (shape[-1] // HD, HD)
    scores = (
        jnp.einsum(
            "...qhd,...khd->...hqk",
            moved_q.reshape(split),
            moved_k.reshape(split),
            preferred_element_type=jnp.float32,
        )
        * scale
    )
    weights = jnp.exp(scores)
    weights = (weights / jnp.sum(weights, -1, keepdims=True)).astype(jnp.bfloat16)
    result = jnp.einsum(
        "...hqk,...khd->...qhd", weights, moved_v.reshape(split), preferred_element_type=jnp.float32
    ).astype(jnp.bfloat16)
    return jnp.moveaxis(result.reshape(shape), -2, dim)


def on_device(tokens, norm1_gain, w_qkv, w_out, norm2_gain, w_up, w_down):
    whole = lax.all_gather(tokens, "col", axis=3, tiled=True)
    frames, rows_h, width, model = whole.shape
    count = frames * rows_h * width
    half = tokens.shape[3]
    wide = whole.astype(jnp.float32).reshape(count, model)
    normed = layer_norm(wide, norm1_gain).astype(jnp.bfloat16)
    stacked = jnp.einsum("rd,sdc->src", normed, w_qkv, preferred_element_type=jnp.float32).astype(
        jnp.bfloat16
    )
    stacked = stacked.reshape(3, frames, rows_h, width, half)
    along_w = attend(stacked[0], stacked[1], stacked[2], 2)
    columns = lax.all_to_all(stacked, "ha", split_axis=3, concat_axis=2, tiled=True)
    along_h_far = attend(columns[0], columns[1], columns[2], 1)
    along_h = lax.all_to_all(along_h_far, "ha", split_axis=1, concat_axis=2, tiled=True)
    lines = lax.all_to_all(stacked, "ta", split_axis=3, concat_axis=1, tiled=True)
    along_t_far = attend(lines[0], lines[1], lines[2], 0)
    along_t = lax.all_to_all(along_t_far, "ta", split_axis=0, concat_axis=2, tiled=True)
    mixed = (
        along_w.astype(jnp.float32) + along_h.astype(jnp.float32) + along_t.astype(jnp.float32)
    ).astype(jnp.bfloat16)
    terms = jnp.dot(mixed.reshape(count, half), w_out, preferred_element_type=jnp.float32)
    offset = lax.axis_index("col") * half
    summed = lax.psum(terms, "col")
    first_full = wide + summed
    second = layer_norm(first_full, norm2_gain).astype(jnp.bfloat16)
    first = lax.dynamic_slice_in_dim(first_full, offset, half, 1)
    upper = jnp.dot(
        second, lax.all_gather(w_up, "ha", axis=0, tiled=True), preferred_element_type=jnp.float32
    )
    hidden = jax.nn.gelu(upper, approximate=False).astype(jnp.bfloat16)
    down_terms = jnp.dot(
        hidden, lax.all_gather(w_down, "ha", axis=1, tiled=True), preferred_element_type=jnp.float32
    )
    down_share = lax.psum_scatter(
        down_terms.astype(jnp.bfloat16), "col", scatter_dimension=1, tiled=True
    ).astype(jnp.float32)
    return (first + down_share).astype(jnp.bfloat16).reshape(frames, rows_h, width, half)


F32 = jnp.float32
BF = jnp.bfloat16


def norm_rows(parts, gain_ref, out_ref, rows):
    half = parts[0].shape[-1]
    model = 2 * half
    total = jnp.sum(parts[0], -1, keepdims=True) + jnp.sum(parts[1], -1, keepdims=True)
    mean = total * (1.0 / model)
    centred = [part - mean for part in parts]
    spread = sum(jnp.sum(part * part, -1, keepdims=True) for part in centred) * (1.0 / model)
    factor = lax.rsqrt(spread + EPS)
    for at, part in enumerate(centred):
        gain = gain_ref[at * half : (at + 1) * half].reshape(1, half)
        out_ref[rows, at * half : (at + 1) * half] = (part * factor * gain).astype(BF)


def attend_pair(query, keys, values, mask):
    count = query.shape[0]
    low = lax.broadcasted_iota(jnp.int32, query.shape, 1) < HD
    zero = jnp.zeros_like(query)
    both = jnp.concatenate([jnp.where(low, query, zero), jnp.where(low, zero, query)], 0)
    scores = lax.dot_general(both, keys, (((1,), (1,)), ((), ())), preferred_element_type=F32)
    weights = jnp.where(mask, jnp.exp(scores), 0.0)
    ones = jnp.ones((keys.shape[0], 128), BF)
    sums = jnp.dot(weights.astype(BF), ones, preferred_element_type=F32)
    probs = (weights / sums).astype(BF)
    found = jnp.dot(probs, values, preferred_element_type=F32)
    return jnp.where(low, found[:count], found[count:]).astype(BF).astype(F32)


def block_kernel(
    sizes, tok, gain1, wqkv_hbm, wout_hbm, gain2, wup_hbm, wdn_hbm, out,
    own, sendb, strip, nrm, qkv, found, heads_w, backb, back, mix, first,
    wq, wo, wu, wd, hid, downb, downr, wide,
    sem_l, s_tok, r_tok, s_col, r_col, s_fwd, r_fwd, s_ret, r_ret,
    s_z, r_z, s_p, r_p, s_mix, r_mix, s_dn, r_dn,
):
    n_g, n_ha, n_ta = sizes
    g, z, t, c = (lax.axis_index(name) for name in ("groups", "ha", "ta", "col"))
    oc = 1 - c
    me = t * n_ha + z
    half = tok.shape[2]
    quarter = t * n_g + g
    partner = {"col": oc}

    def remote(src, dst, send, recv, to):
        return pltpu.make_async_remote_copy(
            src_ref=src, dst_ref=dst, send_sem=send, recv_sem=recv,
            device_id=to, device_id_type=pl.DeviceIdType.MESH,
        )

    moves = [(dt, dz) for dt in range(n_ta) for dz in range(n_ha) if dt or dz]
    plane = [(dt, dg) for dt in range(n_ta) for dg in range(n_g) if dt or dg]

    def other(dt, dz):
        return lax.rem(t + dt, n_ta), lax.rem(z + dz, n_ha)

    barrier = pltpu.get_barrier_semaphore()
    for dt, dz in moves:
        to_t, to_z = other(dt, dz)
        pl.semaphore_signal(barrier, inc=1, device_id={"ha": to_z, "ta": to_t}, device_id_type=pl.DeviceIdType.MESH)
    pl.semaphore_signal(barrier, inc=1, device_id=partner, device_id_type=pl.DeviceIdType.MESH)
    for dt, dg in plane:
        if dg:
            to = {"groups": lax.rem(g + dg, n_g), "ta": lax.rem(t + dt, n_ta)}
            pl.semaphore_signal(barrier, inc=1, device_id=to, device_id_type=pl.DeviceIdType.MESH)

    local = [
        pltpu.make_async_copy(wdn_hbm, wd.at[z], sem_l.at[0]),
        pltpu.make_async_copy(wqkv_hbm, wq, sem_l.at[1]),
        pltpu.make_async_copy(wout_hbm, wo.at[c], sem_l.at[2]),
        pltpu.make_async_copy(wup_hbm, wu.at[z], sem_l.at[3]),
    ]
    for copy in local:
        copy.start()

    lines = tok.shape[0]
    tokens = tok[...].astype(F32)
    narrow = tok.shape[1] // (n_ha * n_ta)
    for s in range(n_ha * n_ta):
        cut = tokens[:, s * narrow : (s + 1) * narrow, :]
        sendb[s] = cut.reshape(lines * narrow, half).astype(BF)
    own[c] = tok[...]
    strip[c, me] = sendb[me]

    n_sig = len(moves) + 1 + sum(1 for dt, dg in plane if dg)
    pl.semaphore_wait(barrier, n_sig)

    own_send = remote(own.at[c], own.at[c], s_col.at[0], r_col.at[0], partner)
    own_send.start()
    sends = []
    for at, (dt, dz) in enumerate(moves):
        to_t, to_z = other(dt, dz)
        copy = remote(sendb.at[to_t * n_ha + to_z], strip.at[c, me], s_tok.at[at], r_tok.at[at], {"ha": to_z, "ta": to_t})
        copy.start()
        sends.append(copy)
    forward = remote(strip.at[c, me], strip.at[c, me], s_fwd.at[len(moves)], r_fwd.at[len(moves)], partner)
    forward.start()
    sends.append(forward)

    held, given = (wu, wd), (wup_hbm, wdn_hbm)
    when_sends = []
    near = [{"groups": lax.rem(g + 1, n_g)}, {"ta": lax.rem(t + 1, n_ta)}]

    def line_copy(kind, way, k, shard):
        at = 0 if way > 0 else 1
        source = given[kind].at[quarter] if k == 1 else held[kind].at[shard, quarter]
        to = {"ha": lax.rem(z + way + n_ha, n_ha)}
        return remote(source, held[kind].at[shard, quarter], s_z.at[kind, at, k - 1], r_z.at[kind, at, k - 1], to)

    def plane_copy(kind, shard, at):
        sides = near if kind == 0 else near[::-1]
        flip_g = lax.rem(g + 1, n_g) + t * n_g
        flip_t = lax.rem(t + 1, n_ta) * n_g + g
        theirs = flip_g if kind == 0 else flip_t
        piece = held[kind].at[shard, theirs if at == 2 else quarter]
        return remote(piece, piece, s_p.at[kind, shard, at], r_p.at[kind, shard, at], sides[min(at, 1)])

    def plane_landing(kind, shard, at):
        flip_g = lax.rem(g + 1, n_g) + t * n_g
        flip_t = lax.rem(t + 1, n_ta) * n_g + g
        flip_both = lax.rem(t + 1, n_ta) * n_g + lax.rem(g + 1, n_g)
        first_of = (flip_g, flip_t, flip_both) if kind == 0 else (flip_t, flip_g, flip_both)
        piece = held[kind].at[shard, first_of[at]]
        return remote(piece, piece, s_p.at[kind, shard, at], r_p.at[kind, shard, at], near[0])

    def starts_when(cond, copy):
        @pl.when(cond)
        def _():
            copy.start()

        when_sends.append((cond, copy))

    def line_first(kind):
        for way in (1, -1):
            ahead = z + way
            starts_when((ahead >= 0) & (ahead < n_ha), line_copy(kind, way, 1, z))

    def line_step(kind, k):
        for way in (1, -1):
            shard = z - way * k
            ahead = z + way
            here = (shard >= 0) & (shard < n_ha)
            safe = lax.rem(shard + n_ha, n_ha)
            landing = held[kind].at[safe, quarter]
            at = 0 if way > 0 else 1

            @pl.when(here)
            def _():
                remote(landing, landing, s_z.at[kind, at, k - 1], r_z.at[kind, at, k - 1], partner).wait_recv()

            if k < n_ha - 1:
                starts_when(here & (ahead >= 0) & (ahead < n_ha), line_copy(kind, way, k + 1, safe))
            for side in range(2):
                starts_when(here, plane_copy(kind, safe, side))

    def plane_step(kind):
        for d in range(1, n_ha):
            shard = lax.rem(z + d, n_ha)
            plane_landing(kind, shard, 0).wait_recv()
            copy = plane_copy(kind, shard, 2)
            copy.start()
            sends.append(copy)

    def plane_wait(kind):
        for d in range(1, n_ha):
            shard = lax.rem(z + d, n_ha)
            plane_landing(kind, shard, 1).wait_recv()
            plane_landing(kind, shard, 2).wait_recv()

    line_first(0)
    line_first(1)
    local[1].wait()
    local[2].wait()
    wo_send = remote(wo.at[c], wo.at[c], s_col.at[1], r_col.at[1], partner)
    wo_send.start()

    def project():
        for i in range(3):
            value = jnp.dot(nrm[...], wq[i], preferred_element_type=F32)
            if i == 0:
                value = value.astype(BF).astype(F32) * (1.0 / math.sqrt(HD))
            qkv[i] = value.astype(BF).reshape(qkv.shape[1:])

    count = lines * tok.shape[1]
    block = 128
    rows_at = lax.rem(lax.broadcasted_iota(jnp.int32, (2 * block, block), 0), block)
    cols_at = lax.broadcasted_iota(jnp.int32, (2 * block, block), 1)
    pairs = half // 128

    own_send.wait()
    norm_rows(
        [own[0].reshape(count, half).astype(F32), own[1].reshape(count, half).astype(F32)],
        gain1, nrm, slice(None),
    )
    project()
    width = tok.shape[1]
    mask_w = rows_at // width == cols_at // width
    flat = qkv.reshape(3, count // block, block, half)

    def along_w(b, carry):
        for p in range(pairs):
            lanes = pl.ds(p * 128, 128)
            heads_w[b, :, lanes] = attend_pair(flat[0, b, :, lanes], flat[1, b, :, lanes], flat[2, b, :, lanes], mask_w)
        return carry

    lax.fori_loop(0, count // block, along_w, 0)

    for at, (dt, dz) in enumerate(moves):
        from_t, from_z = lax.rem(t + n_ta - dt, n_ta), lax.rem(z + n_ha - dz, n_ha)
        src = from_t * n_ha + from_z
        remote(sendb.at[0], strip.at[c, src], s_tok.at[at], r_tok.at[at], partner).wait_recv()
        copy = remote(strip.at[c, src], strip.at[c, src], s_fwd.at[at], r_fwd.at[at], partner)
        copy.start()
        sends.append(copy)
    for at, (dt, dz) in enumerate(moves + [(0, 0)]):
        from_t, from_z = lax.rem(t + n_ta - dt, n_ta), lax.rem(z + n_ha - dz, n_ha)
        src = from_t * n_ha + from_z
        remote(strip.at[oc, src], strip.at[oc, src], s_fwd.at[at], r_fwd.at[at], partner).wait_recv()
    line_step(0, 1)
    norm_rows(
        [strip[0].reshape(count, half).astype(F32), strip[1].reshape(count, half).astype(F32)],
        gain1, nrm, slice(None),
    )
    project()
    line_step(0, 2)
    frames = 2
    mask_h = lax.rem(rows_at, narrow) == lax.rem(cols_at, narrow)
    same = lines // frames * narrow
    mask_t = lax.rem(rows_at, same) == lax.rem(cols_at, same)

    def along_h(b, carry):
        tt, ff = b // frames, lax.rem(b, frames)
        for p in range(pairs):
            lanes = pl.ds(p * 128, 128)
            q, k, v = (qkv[i, tt, :, ff, :, lanes].reshape(block, 128) for i in range(3))
            found[tt, :, ff, :, lanes] = attend_pair(q, k, v, mask_h).reshape(n_ha, same, 128)
        return carry

    def along_t(zz, carry):
        for p in range(pairs):
            lanes = pl.ds(p * 128, 128)
            q, k, v = (qkv[i, :, zz, :, :, lanes].reshape(block, 128) for i in range(3))
            more = attend_pair(q, k, v, mask_t).reshape(n_ta, frames, same, 128)
            backb[:, zz, :, :, lanes] = (found[:, zz, :, :, lanes] + more).astype(BF)
        return carry

    lax.fori_loop(0, n_ta * frames, along_h, 0)
    line_step(1, 1)
    line_step(0, 3)
    lax.fori_loop(0, n_ha, along_t, 0)

    for at, (dt, dz) in enumerate(moves):
        to_t, to_z = other(dt, dz)
        copy = remote(backb.at[to_t, to_z], back.at[t, z], s_ret.at[at], r_ret.at[at], {"ha": to_z, "ta": to_t})
        copy.start()
        sends.append(copy)
    back[t, z] = backb[t, z]

    line_step(1, 2)
    plane_step(0)
    for at, (dt, dz) in enumerate(moves):
        from_t, from_z = lax.rem(t + n_ta - dt, n_ta), lax.rem(z + n_ha - dz, n_ha)
        remote(back.at[from_t, from_z], back.at[from_t, from_z], s_ret.at[at], r_ret.at[at], partner).wait_recv()
    for s in range(n_ha * n_ta):
        piece = back[s // n_ha, s % n_ha].astype(F32)
        wide[:, s * narrow : (s + 1) * narrow, :] = piece.reshape(lines, narrow, half)
    mix[c] = (wide[...].reshape(count, half) + heads_w[...].reshape(count, half)).astype(BF)
    mix_send = remote(mix.at[c], mix.at[c], s_mix.at[0], r_mix.at[0], partner)
    mix_send.start()
    line_step(1, 3)
    wo_send.wait()
    first[...] = jnp.dot(mix[c], wo[c], preferred_element_type=F32)
    mix_send.wait()
    first[...] += jnp.dot(mix[oc], wo[oc], preferred_element_type=F32)
    parts = []
    for i in range(2):
        cols = slice(i * half, (i + 1) * half)
        part = own[i].reshape(count, half).astype(F32) + first[:, cols]
        first[:, cols] = part
        parts.append(part)
    norm_rows(parts, gain2, nrm, slice(None))

    plane_step(1)
    local[3].wait()
    plane_wait(0)
    units = wu.shape[3]
    step = 256

    def feed(u, carry):
        cols = pl.ds(pl.multiple_of(u * step, step), step)
        up = jnp.dot(nrm[...], wu[:, :, :, cols].reshape(2 * half, step), preferred_element_type=F32)
        up = 0.5 * up * (1.0 + lax.erf(up * math.sqrt(0.5)))
        hid[:, cols] = up.astype(BF)
        return carry

    lax.fori_loop(0, units // step, feed, 0)

    local[0].wait()
    plane_wait(1)
    here = pl.ds(pl.multiple_of(c * half, 128), half)
    share = n_ha // 2

    def down_dot(rows, side):
        weights = wd[pl.ds(side * share, share)].reshape(half, units)
        return lax.dot_general(hid[rows, :], weights, (((1,), (1,)), ((), ())), preferred_element_type=F32)

    n_rows = 2
    tall = count // n_rows
    down = []
    for r in range(n_rows):
        rows = slice(r * tall, (r + 1) * tall)
        downb[r] = down_dot(rows, oc).astype(BF)
        copy = remote(downb.at[r], downr.at[r], s_dn.at[r], r_dn.at[r], partner)
        copy.start()
        down.append(copy)
    for r in range(n_rows):
        rows = slice(r * tall, (r + 1) * tall)
        mine = down_dot(rows, c)
        down[r].wait_recv()
        mine = mine + downr[r].astype(F32)
        out[rows, :] = (mine + first[rows, here]).astype(BF)
    for copy in down + sends:
        copy.wait_send()
    for cond, copy in when_sends:

        @pl.when(cond)
        def _():
            copy.wait_send()


def on_device_fused(sizes, tokens, norm1_gain, w_qkv, w_out, norm2_gain, w_up, w_down):
    n_g, n_ha, n_ta = sizes
    frames, rows_h, width, half = tokens.shape
    lines = frames * rows_h
    count = lines * width
    strips = n_ha * n_ta
    narrow = width // strips
    same = rows_h * narrow
    units = w_up.shape[1]
    dma = pltpu.SemaphoreType.DMA
    vm = pltpu.VMEM
    n_moves = strips - 1
    scratch = [
        vm((2, lines, width, half), BF),
        vm((strips, lines * narrow, half), BF),
        vm((2, strips, lines * narrow, half), BF),
        vm((count, 2 * half), BF),
        vm((3, n_ta, n_ha, frames, same, half), BF),
        vm((n_ta, n_ha, frames, same, half), F32),
        vm((count // 128, 128, half), F32),
        vm((n_ta, n_ha, frames, same, half), BF),
        vm((n_ta, n_ha, frames, same, half), BF),
        vm((2, count, half), BF),
        vm((count, 2 * half), F32),
        vm((3, 2 * half, half), BF),
        vm((2, half, 2 * half), BF),
        vm((n_ha, 4, w_up.shape[0] // 4, units), BF),
        vm((n_ha, 4, w_up.shape[0] // 4, units), BF),
        vm((count, units), BF),
        vm((2, count // 2, half), BF),
        vm((2, count // 2, half), BF),
        vm((lines, width, half), F32),
        dma((4,)),
        dma((n_moves,)), dma((n_moves,)),
        dma((2,)), dma((2,)),
        dma((strips,)), dma((strips,)),
        dma((n_moves,)), dma((n_moves,)),
        dma((2, 2, n_ha)), dma((2, 2, n_ha)),
        dma((2, n_ha, 3)), dma((2, n_ha, 3)),
        dma((1,)), dma((1,)),
        dma((2,)), dma((2,)),
    ]
    in_vmem = pl.BlockSpec(memory_space=pltpu.VMEM)
    anywhere = pl.BlockSpec(memory_space=pl.ANY)
    result = pl.pallas_call(
        functools.partial(block_kernel, sizes),
        out_shape=jax.ShapeDtypeStruct((count, half), BF),
        in_specs=[in_vmem, in_vmem, anywhere, anywhere, in_vmem, anywhere, anywhere],
        out_specs=in_vmem,
        scratch_shapes=scratch,
        compiler_params=pltpu.CompilerParams(
            collective_id=0, has_side_effects=True, vmem_limit_bytes=56 * 2**20
        ),
    )(
        tokens.reshape(lines, width, half), norm1_gain, w_qkv, w_out,
        norm2_gain, w_up.reshape(4, w_up.shape[0] // 4, units),
        w_down.T.reshape(4, w_up.shape[0] // 4, units),
    )
    return result.reshape(frames, rows_h, width, half)


def fits(mesh):
    shape = mesh.shape
    return shape["groups"] == 2 and shape["ta"] == 2 and shape["ha"] == 4 and shape["col"] == 2


def solution(mesh):
    placed = (
        P(("groups", "ta"), "ha", None, "col"),
        P(),
        P(None, None, "col"),
        P("col", None),
        P(),
        P("ha", "col"),
        P("col", "ha"),
    )
    body = on_device
    if fits(mesh):
        body = functools.partial(on_device_fused, (mesh.shape["groups"], mesh.shape["ha"], mesh.shape["ta"]))
    return jax.shard_map(
        body,
        mesh=mesh,
        in_specs=placed,
        out_specs=P(("groups", "ta"), "ha", None, "col"),
        check_vma=False,
    )
```

```python
import functools
import math

import jax
import jax.numpy as jnp
from jax import lax
from jax.experimental import pallas as pl
from jax.experimental.pallas import tpu as pltpu
from jax.sharding import PartitionSpec as P

HD = 64


EPS = 1e-05


def layer_norm(values, gain):
    mean = jnp.mean(values, -1, keepdims=True)
    centred = values - mean
    spread = jnp.mean(centred * centred, -1, keepdims=True)
    return centred * lax.rsqrt(spread + EPS) * gain


def attend(query, keys, values, dim):
    scale = 1.0 / math.sqrt(HD)
    moved_q = jnp.moveaxis(query, dim, -2)
    moved_k = jnp.moveaxis(keys, dim, -2)
    moved_v = jnp.moveaxis(values, dim, -2)
    shape = moved_q.shape
    split = shape[:-1] + (shape[-1] // HD, HD)
    scores = (
        jnp.einsum(
            "...qhd,...khd->...hqk",
            moved_q.reshape(split),
            moved_k.reshape(split),
            preferred_element_type=jnp.float32,
        )
        * scale
    )
    weights = jnp.exp(scores)
    weights = (weights / jnp.sum(weights, -1, keepdims=True)).astype(jnp.bfloat16)
    result = jnp.einsum(
        "...hqk,...khd->...qhd", weights, moved_v.reshape(split), preferred_element_type=jnp.float32
    ).astype(jnp.bfloat16)
    return jnp.moveaxis(result.reshape(shape), -2, dim)


def on_device(tokens, norm1_gain, w_qkv, w_out, norm2_gain, w_up, w_down):
    whole = lax.all_gather(tokens, "col", axis=3, tiled=True)
    frames, rows_h, width, model = whole.shape
    count = frames * rows_h * width
    half = tokens.shape[3]
    wide = whole.astype(jnp.float32).reshape(count, model)
    normed = layer_norm(wide, norm1_gain).astype(jnp.bfloat16)
    stacked = jnp.einsum("rd,sdc->src", normed, w_qkv, preferred_element_type=jnp.float32).astype(
        jnp.bfloat16
    )
    stacked = stacked.reshape(3, frames, rows_h, width, half)
    along_w = attend(stacked[0], stacked[1], stacked[2], 2)
    columns = lax.all_to_all(stacked, "ha", split_axis=3, concat_axis=2, tiled=True)
    along_h_far = attend(columns[0], columns[1], columns[2], 1)
    along_h = lax.all_to_all(along_h_far, "ha", split_axis=1, concat_axis=2, tiled=True)
    lines = lax.all_to_all(stacked, "ta", split_axis=3, concat_axis=1, tiled=True)
    along_t_far = attend(lines[0], lines[1], lines[2], 0)
    along_t = lax.all_to_all(along_t_far, "ta", split_axis=0, concat_axis=2, tiled=True)
    mixed = (
        along_w.astype(jnp.float32) + along_h.astype(jnp.float32) + along_t.astype(jnp.float32)
    ).astype(jnp.bfloat16)
    terms = jnp.dot(mixed.reshape(count, half), w_out, preferred_element_type=jnp.float32)
    offset = lax.axis_index("col") * half
    summed = lax.psum(terms, "col")
    first_full = wide + summed
    second = layer_norm(first_full, norm2_gain).astype(jnp.bfloat16)
    first = lax.dynamic_slice_in_dim(first_full, offset, half, 1)
    upper = jnp.dot(
        second, lax.all_gather(w_up, "ha", axis=0, tiled=True), preferred_element_type=jnp.float32
    )
    hidden = jax.nn.gelu(upper, approximate=False).astype(jnp.bfloat16)
    down_terms = jnp.dot(
        hidden, lax.all_gather(w_down, "ha", axis=1, tiled=True), preferred_element_type=jnp.float32
    )
    down_share = lax.psum_scatter(
        down_terms.astype(jnp.bfloat16), "col", scatter_dimension=1, tiled=True
    ).astype(jnp.float32)
    return (first + down_share).astype(jnp.bfloat16).reshape(frames, rows_h, width, half)


F32 = jnp.float32
BF = jnp.bfloat16


def norm_rows(parts, gain_ref, out_ref, rows):
    half = parts[0].shape[-1]
    model = 2 * half
    total = jnp.sum(parts[0], -1, keepdims=True) + jnp.sum(parts[1], -1, keepdims=True)
    mean = total * (1.0 / model)
    centred = [part - mean for part in parts]
    spread = sum(jnp.sum(part * part, -1, keepdims=True) for part in centred) * (1.0 / model)
    factor = lax.rsqrt(spread + EPS)
    for at, part in enumerate(centred):
        gain = gain_ref[at * half : (at + 1) * half].reshape(1, half)
        out_ref[rows, at * half : (at + 1) * half] = (part * factor * gain).astype(BF)


def attend_pair(query, keys, values, mask):
    count = query.shape[0]
    low = lax.broadcasted_iota(jnp.int32, query.shape, 1) < HD
    zero = jnp.zeros_like(query)
    both = jnp.concatenate([jnp.where(low, query, zero), jnp.where(low, zero, query)], 0)
    scores = lax.dot_general(both, keys, (((1,), (1,)), ((), ())), preferred_element_type=F32)
    weights = jnp.where(mask, jnp.exp(scores), 0.0)
    ones = jnp.ones((keys.shape[0], 128), BF)
    sums = jnp.dot(weights.astype(BF), ones, preferred_element_type=F32)
    probs = (weights / sums).astype(BF)
    found = jnp.dot(probs, values, preferred_element_type=F32)
    return jnp.where(low, found[:count], found[count:]).astype(BF).astype(F32)


def block_kernel(
    sizes, tok, gain1, wqkv_hbm, wout_hbm, gain2, wup_hbm, wdn_hbm, out,
    own, sendb, strip, nrm, qkv, found, heads_w, backb, back, mix, first,
    wq, wo, wu, wd, hid, downb, downr, wide,
    sem_l, s_tok, r_tok, s_col, r_col, s_fwd, r_fwd, s_ret, r_ret,
    s_z, r_z, s_p, r_p, s_mix, r_mix, s_dn, r_dn,
):
    n_g, n_ha, n_ta = sizes
    g, z, t, c = (lax.axis_index(name) for name in ("groups", "ha", "ta", "col"))
    oc = 1 - c
    me = t * n_ha + z
    half = tok.shape[2]
    quarter = t * n_g + g
    partner = {"col": oc}

    def remote(src, dst, send, recv, to):
        return pltpu.make_async_remote_copy(
            src_ref=src, dst_ref=dst, send_sem=send, recv_sem=recv,
            device_id=to, device_id_type=pl.DeviceIdType.MESH,
        )

    moves = [(dt, dz) for dt in range(n_ta) for dz in range(n_ha) if dt or dz]
    plane = [(dt, dg) for dt in range(n_ta) for dg in range(n_g) if dt or dg]

    def other(dt, dz):
        return lax.rem(t + dt, n_ta), lax.rem(z + dz, n_ha)

    barrier = pltpu.get_barrier_semaphore()
    for dt, dz in moves:
        to_t, to_z = other(dt, dz)
        pl.semaphore_signal(barrier, inc=1, device_id={"ha": to_z, "ta": to_t}, device_id_type=pl.DeviceIdType.MESH)
    pl.semaphore_signal(barrier, inc=1, device_id=partner, device_id_type=pl.DeviceIdType.MESH)
    for dt, dg in plane:
        if dg:
            to = {"groups": lax.rem(g + dg, n_g), "ta": lax.rem(t + dt, n_ta)}
            pl.semaphore_signal(barrier, inc=1, device_id=to, device_id_type=pl.DeviceIdType.MESH)

    local = [
        pltpu.make_async_copy(wdn_hbm, wd.at[z], sem_l.at[0]),
        pltpu.make_async_copy(wqkv_hbm, wq, sem_l.at[1]),
        pltpu.make_async_copy(wout_hbm, wo.at[c], sem_l.at[2]),
        pltpu.make_async_copy(wup_hbm, wu.at[z], sem_l.at[3]),
    ]
    for copy in local:
        copy.start()

    lines = tok.shape[0]
    tokens = tok[...].astype(F32)
    narrow = tok.shape[1] // (n_ha * n_ta)
    for s in range(n_ha * n_ta):
        cut = tokens[:, s * narrow : (s + 1) * narrow, :]
        sendb[s] = cut.reshape(lines * narrow, half).astype(BF)
    own[c] = tok[...]
    strip[c, me] = sendb[me]

    n_sig = len(moves) + 1 + sum(1 for dt, dg in plane if dg)
    pl.semaphore_wait(barrier, n_sig)

    own_send = remote(own.at[c], own.at[c], s_col.at[0], r_col.at[0], partner)
    own_send.start()
    sends = []
    for at, (dt, dz) in enumerate(moves):
        to_t, to_z = other(dt, dz)
        copy = remote(sendb.at[to_t * n_ha + to_z], strip.at[c, me], s_tok.at[at], r_tok.at[at], {"ha": to_z, "ta": to_t})
        copy.start()
        sends.append(copy)
    forward = remote(strip.at[c, me], strip.at[c, me], s_fwd.at[len(moves)], r_fwd.at[len(moves)], partner)
    forward.start()
    sends.append(forward)

    held, given = (wu, wd), (wup_hbm, wdn_hbm)
    when_sends = []
    near = [{"groups": lax.rem(g + 1, n_g)}, {"ta": lax.rem(t + 1, n_ta)}]

    def line_copy(kind, way, k, shard):
        at = 0 if way > 0 else 1
        source = given[kind].at[quarter] if k == 1 else held[kind].at[shard, quarter]
        to = {"ha": lax.rem(z + way + n_ha, n_ha)}
        return remote(source, held[kind].at[shard, quarter], s_z.at[kind, at, k - 1], r_z.at[kind, at, k - 1], to)

    def plane_copy(kind, shard, at):
        sides = near if kind == 0 else near[::-1]
        flip_g = lax.rem(g + 1, n_g) + t * n_g
        flip_t = lax.rem(t + 1, n_ta) * n_g + g
        theirs = flip_g if kind == 0 else flip_t
        piece = held[kind].at[shard, theirs if at == 2 else quarter]
        return remote(piece, piece, s_p.at[kind, shard, at], r_p.at[kind, shard, at], sides[min(at, 1)])

    def plane_landing(kind, shard, at):
        flip_g = lax.rem(g + 1, n_g) + t * n_g
        flip_t = lax.rem(t + 1, n_ta) * n_g + g
        flip_both = lax.rem(t + 1, n_ta) * n_g + lax.rem(g + 1, n_g)
        first_of = (flip_g, flip_t, flip_both) if kind == 0 else (flip_t, flip_g, flip_both)
        piece = held[kind].at[shard, first_of[at]]
        return remote(piece, piece, s_p.at[kind, shard, at], r_p.at[kind, shard, at], near[0])

    def starts_when(cond, copy):
        @pl.when(cond)
        def _():
            copy.start()

        when_sends.append((cond, copy))

    def line_first(kind):
        for way in (1, -1):
            ahead = z + way
            starts_when((ahead >= 0) & (ahead < n_ha), line_copy(kind, way, 1, z))

    def line_step(kind, k):
        for way in (1, -1):
            shard = z - way * k
            ahead = z + way
            here = (shard >= 0) & (shard < n_ha)
            safe = lax.rem(shard + n_ha, n_ha)
            landing = held[kind].at[safe, quarter]
            at = 0 if way > 0 else 1

            @pl.when(here)
            def _():
                remote(landing, landing, s_z.at[kind, at, k - 1], r_z.at[kind, at, k - 1], partner).wait_recv()

            if k < n_ha - 1:
                starts_when(here & (ahead >= 0) & (ahead < n_ha), line_copy(kind, way, k + 1, safe))
            for side in range(2):
                starts_when(here, plane_copy(kind, safe, side))

    def plane_step(kind, k):
        for way in (1, -1):
            shard = z - way * k
            here = (shard >= 0) & (shard < n_ha)
            safe = lax.rem(shard + n_ha, n_ha)
            landing = plane_landing(kind, safe, 0)

            @pl.when(here)
            def _():
                landing.wait_recv()

            starts_when(here, plane_copy(kind, safe, 2))

    def plane_wait(kind):
        for d in range(1, n_ha):
            shard = lax.rem(z + d, n_ha)
            plane_landing(kind, shard, 1).wait_recv()
            plane_landing(kind, shard, 2).wait_recv()

    line_first(0)
    local[1].wait()
    local[2].wait()
    wo_send = remote(wo.at[c], wo.at[c], s_col.at[1], r_col.at[1], partner)
    wo_send.start()

    def project():
        for i in range(3):
            value = jnp.dot(nrm[...], wq[i], preferred_element_type=F32)
            if i == 0:
                value = value.astype(BF).astype(F32) * (1.0 / math.sqrt(HD))
            qkv[i] = value.astype(BF).reshape(qkv.shape[1:])

    count = lines * tok.shape[1]
    block = 128
    rows_at = lax.rem(lax.broadcasted_iota(jnp.int32, (2 * block, block), 0), block)
    cols_at = lax.broadcasted_iota(jnp.int32, (2 * block, block), 1)
    pairs = half // 128

    own_send.wait()
    norm_rows(
        [own[0].reshape(count, half).astype(F32), own[1].reshape(count, half).astype(F32)],
        gain1, nrm, slice(None),
    )
    project()
    line_first(1)
    width = tok.shape[1]
    mask_w = rows_at // width == cols_at // width
    flat = qkv.reshape(3, count // block, block, half)

    def along_w(b, carry):
        for p in range(pairs):
            lanes = pl.ds(p * 128, 128)
            heads_w[b, :, lanes] = attend_pair(flat[0, b, :, lanes], flat[1, b, :, lanes], flat[2, b, :, lanes], mask_w)
        return carry

    lax.fori_loop(0, count // block, along_w, 0, unroll=2)
    line_step(0, 1)

    for at, (dt, dz) in enumerate(moves):
        from_t, from_z = lax.rem(t + n_ta - dt, n_ta), lax.rem(z + n_ha - dz, n_ha)
        src = from_t * n_ha + from_z
        remote(sendb.at[0], strip.at[c, src], s_tok.at[at], r_tok.at[at], partner).wait_recv()
        copy = remote(strip.at[c, src], strip.at[c, src], s_fwd.at[at], r_fwd.at[at], partner)
        copy.start()
        sends.append(copy)
    for at, (dt, dz) in enumerate(moves + [(0, 0)]):
        from_t, from_z = lax.rem(t + n_ta - dt, n_ta), lax.rem(z + n_ha - dz, n_ha)
        src = from_t * n_ha + from_z
        remote(strip.at[oc, src], strip.at[oc, src], s_fwd.at[at], r_fwd.at[at], partner).wait_recv()
    line_step(1, 1)
    norm_rows(
        [strip[0].reshape(count, half).astype(F32), strip[1].reshape(count, half).astype(F32)],
        gain1, nrm, slice(None),
    )
    project()
    line_step(0, 2)
    plane_step(0, 1)
    frames = 2
    mask_h = lax.rem(rows_at, narrow) == lax.rem(cols_at, narrow)
    same = lines // frames * narrow
    mask_t = lax.rem(rows_at, same) == lax.rem(cols_at, same)

    def along_h(b, carry):
        tt, ff = b // frames, lax.rem(b, frames)
        for p in range(pairs):
            lanes = pl.ds(p * 128, 128)
            q, k, v = (qkv[i, tt, :, ff, :, lanes].reshape(block, 128) for i in range(3))
            found[tt, :, ff, :, lanes] = attend_pair(q, k, v, mask_h).reshape(n_ha, same, 128)
        return carry

    def along_t(zz, carry):
        for p in range(pairs):
            lanes = pl.ds(p * 128, 128)
            q, k, v = (qkv[i, :, zz, :, :, lanes].reshape(block, 128) for i in range(3))
            more = attend_pair(q, k, v, mask_t).reshape(n_ta, frames, same, 128)
            backb[:, zz, :, :, lanes] = (found[:, zz, :, :, lanes] + more).astype(BF)
        return carry

    lax.fori_loop(0, n_ta * frames, along_h, 0, unroll=2)
    line_step(1, 2)
    plane_step(1, 1)
    line_step(0, 3)
    lax.fori_loop(0, n_ha, along_t, 0, unroll=2)

    for at, (dt, dz) in enumerate(moves):
        to_t, to_z = other(dt, dz)
        copy = remote(backb.at[to_t, to_z], back.at[t, z], s_ret.at[at], r_ret.at[at], {"ha": to_z, "ta": to_t})
        copy.start()
        sends.append(copy)
    back[t, z] = backb[t, z]
    line_step(1, 3)
    plane_step(0, 2)
    plane_step(0, 3)

    for at, (dt, dz) in enumerate(moves):
        from_t, from_z = lax.rem(t + n_ta - dt, n_ta), lax.rem(z + n_ha - dz, n_ha)
        remote(back.at[from_t, from_z], back.at[from_t, from_z], s_ret.at[at], r_ret.at[at], partner).wait_recv()
    for s in range(n_ha * n_ta):
        piece = back[s // n_ha, s % n_ha].astype(F32)
        wide[:, s * narrow : (s + 1) * narrow, :] = piece.reshape(lines, narrow, half)
    mix[c] = (wide[...].reshape(count, half) + heads_w[...].reshape(count, half)).astype(BF)
    mix_send = remote(mix.at[c], mix.at[c], s_mix.at[0], r_mix.at[0], partner)
    mix_send.start()
    plane_step(1, 2)
    wo_send.wait()
    first[...] = jnp.dot(mix[c], wo[c], preferred_element_type=F32)
    mix_send.wait()
    first[...] += jnp.dot(mix[oc], wo[oc], preferred_element_type=F32)
    parts = []
    for i in range(2):
        cols = slice(i * half, (i + 1) * half)
        part = own[i].reshape(count, half).astype(F32) + first[:, cols]
        first[:, cols] = part
        parts.append(part)
    norm_rows(parts, gain2, nrm, slice(None))

    local[3].wait()
    plane_step(1, 3)
    plane_wait(0)
    units = wu.shape[3]
    step = 256

    def feed(u, carry):
        cols = pl.ds(pl.multiple_of(u * step, step), step)
        up = jnp.dot(nrm[...], wu[:, :, :, cols].reshape(2 * half, step), preferred_element_type=F32)
        up = 0.5 * up * (1.0 + lax.erf(up * math.sqrt(0.5)))
        hid[:, cols] = up.astype(BF)
        return carry

    lax.fori_loop(0, 3, feed, 0)
    lax.fori_loop(3, units // step, feed, 0)
    plane_wait(1)

    local[0].wait()
    here = pl.ds(pl.multiple_of(c * half, 128), half)
    share = n_ha // 2

    def down_dot(rows, side):
        weights = wd[pl.ds(side * share, share)].reshape(half, units)
        return lax.dot_general(hid[rows, :], weights, (((1,), (1,)), ((), ())), preferred_element_type=F32)

    n_rows = 2
    tall = count // n_rows
    down = []
    for r in range(n_rows):
        rows = slice(r * tall, (r + 1) * tall)
        downb[r] = down_dot(rows, oc).astype(BF)
        copy = remote(downb.at[r], downr.at[r], s_dn.at[r], r_dn.at[r], partner)
        copy.start()
        down.append(copy)
    for r in range(n_rows):
        rows = slice(r * tall, (r + 1) * tall)
        mine = down_dot(rows, c)
        down[r].wait_recv()
        mine = mine + downr[r].astype(F32)
        out[rows, :] = (mine + first[rows, here]).astype(BF)
    for copy in down + sends:
        copy.wait_send()
    for cond, copy in when_sends:

        @pl.when(cond)
        def _():
            copy.wait_send()


def on_device_fused(sizes, tokens, norm1_gain, w_qkv, w_out, norm2_gain, w_up, w_down):
    n_g, n_ha, n_ta = sizes
    frames, rows_h, width, half = tokens.shape
    lines = frames * rows_h
    count = lines * width
    strips = n_ha * n_ta
    narrow = width // strips
    same = rows_h * narrow
    units = w_up.shape[1]
    dma = pltpu.SemaphoreType.DMA
    vm = pltpu.VMEM
    n_moves = strips - 1
    scratch = [
        vm((2, lines, width, half), BF),
        vm((strips, lines * narrow, half), BF),
        vm((2, strips, lines * narrow, half), BF),
        vm((count, 2 * half), BF),
        vm((3, n_ta, n_ha, frames, same, half), BF),
        vm((n_ta, n_ha, frames, same, half), F32),
        vm((count // 128, 128, half), F32),
        vm((n_ta, n_ha, frames, same, half), BF),
        vm((n_ta, n_ha, frames, same, half), BF),
        vm((2, count, half), BF),
        vm((count, 2 * half), F32),
        vm((3, 2 * half, half), BF),
        vm((2, half, 2 * half), BF),
        vm((n_ha, 4, w_up.shape[0] // 4, units), BF),
        vm((n_ha, 4, w_up.shape[0] // 4, units), BF),
        vm((count, units), BF),
        vm((2, count // 2, half), BF),
        vm((2, count // 2, half), BF),
        vm((lines, width, half), F32),
        dma((4,)),
        dma((n_moves,)), dma((n_moves,)),
        dma((2,)), dma((2,)),
        dma((strips,)), dma((strips,)),
        dma((n_moves,)), dma((n_moves,)),
        dma((2, 2, n_ha)), dma((2, 2, n_ha)),
        dma((2, n_ha, 3)), dma((2, n_ha, 3)),
        dma((1,)), dma((1,)),
        dma((2,)), dma((2,)),
    ]
    in_vmem = pl.BlockSpec(memory_space=pltpu.VMEM)
    anywhere = pl.BlockSpec(memory_space=pl.ANY)
    result = pl.pallas_call(
        functools.partial(block_kernel, sizes),
        out_shape=jax.ShapeDtypeStruct((count, half), BF),
        in_specs=[in_vmem, in_vmem, anywhere, anywhere, in_vmem, anywhere, anywhere],
        out_specs=in_vmem,
        scratch_shapes=scratch,
        compiler_params=pltpu.CompilerParams(
            collective_id=0, has_side_effects=True, vmem_limit_bytes=56 * 2**20
        ),
    )(
        tokens.reshape(lines, width, half), norm1_gain, w_qkv, w_out,
        norm2_gain, w_up.reshape(4, w_up.shape[0] // 4, units),
        w_down.T.reshape(4, w_up.shape[0] // 4, units),
    )
    return result.reshape(frames, rows_h, width, half)


def fits(mesh):
    shape = mesh.shape
    return shape["groups"] == 2 and shape["ta"] == 2 and shape["ha"] == 4 and shape["col"] == 2


def solution(mesh):
    placed = (
        P(("groups", "ta"), "ha", None, "col"),
        P(),
        P(None, None, "col"),
        P("col", None),
        P(),
        P("ha", "col"),
        P("col", "ha"),
    )
    body = on_device
    if fits(mesh):
        body = functools.partial(on_device_fused, (mesh.shape["groups"], mesh.shape["ha"], mesh.shape["ta"]))
    return jax.shard_map(
        body,
        mesh=mesh,
        in_specs=placed,
        out_specs=P(("groups", "ta"), "ha", None, "col"),
        check_vma=False,
    )
```
